256 devices in a mesh: wide: 32 (over x, z), narrow: 8 (over y, core).
Axes of the slice: x: 4, y: 4, z: 8, core: 2. Of those that a mesh axis runs over, the one named last changes fastest.
Arguments:
- user_vectors: bfloat16 [32768, 64], P('wide'), may hold values from -230 to 230
- campaigns: bfloat16 [51200, 64], P('narrow'), may hold values from -5 to 5
- campaign_bids: float32 [51200], P('narrow'), may hold values from 0.5 to 2
- spend_targets: float32 [51200, 96], P(('narrow', 'wide')), may hold values from 0.002 to 0.02
- dual_prices: float32 [51200, 96], P(('narrow', 'wide')), may hold values from 0.3 to 1.5
- slot_index: int32 [32768], P('wide'), may hold values from 0 to 95
- reserve: float32 [32768], P('wide'), may hold values from 12 to 20
Outputs:
- paced_duals: float32 [51200, 96], P(('narrow', 'wide'))
- fill_rate: float32 [32768], P('wide')
The draws below stay inside these ranges and needn't reach their ends.
All inputs are finite; a program needn't handle non-finite values.
Results may differ from the reference program's by a relative error of at most 0.0029.
Values may be sent and summed in bfloat16 or wider, within the bound.
No kernel may reach another device: no remote copies, remote signals or barrier semaphores. Data moves between devices by JAX's collectives and lax.ppermute only.
A program may use at most 128 MiB of HBM per device.

```python
import math
import jax
import jax.numpy as jnp
from jax import lax

E = 64
SLOTS = 96
ITERS = 2
C = 51200
I = 32768


def campaign_base(key):
    return jnp.clip(jax.random.normal(key, (C, E), jnp.float32), -4.0, 4.0)


def draw_campaigns(key, part):
    base_field = campaign_base(key)
    key = jax.random.fold_in(key, 11)
    jitter_noise = 0.08 * E / 64.0 * jax.random.normal(key, (C, E), jnp.float32)
    row_index = jnp.arange(C)
    paired = (row_index % 2 == 1) & (row_index // 2 % 64 == 0)
    base_field = jnp.where(paired[:, None], jnp.roll(base_field, 1, axis=0) + jitter_noise, base_field)
    return base_field.astype(jnp.bfloat16)


def draw_user_vectors(key, part):
    base_field = campaign_base(key)
    key = jax.random.fold_in(key, 23)
    own_key = jax.random.fold_in(key, 0)
    user_draws = jnp.clip(jax.random.normal(own_key, (I, E), jnp.float32), -4.0, 4.0)
    row_index = jnp.arange(I)
    target = row_index // 64 * 128 % C
    strength = jnp.array([8.0, 11.0, 14.0], jnp.float32)[row_index // 64 % 3]
    aligned = strength[:, None] * base_field[target].astype(jnp.bfloat16).astype(jnp.float32)
    user_draws = jnp.where((row_index % 64 == 0)[:, None], aligned, user_draws)
    return user_draws.astype(jnp.bfloat16)


def touch_ends(drawn, key, low, largest):
    place = [jax.random.randint(jax.random.fold_in(key, axis), (), 0, length) for axis, length in enumerate(drawn.shape)]
    main_axis = drawn.shape.index(max(drawn.shape))
    next_to = place[:main_axis] + [(place[main_axis] + 1) % drawn.shape[main_axis]] + place[main_axis + 1:]
    return drawn.at[tuple(place)].set(low).at[tuple(next_to)].set(largest)


def level_of(rng, extent, cuts, smallest, largest):
    gain, own = 1.0, jax.random.fold_in(rng, 6)
    for position, blocks in cuts:
        steps = jnp.exp(jax.random.uniform(jax.random.fold_in(own, position), (blocks,), jnp.float32, smallest / len(cuts), largest / len(cuts)))
        gain = gain * jnp.repeat(steps, extent[position] // blocks).reshape([-1 if axis == position else 1 for axis in range(len(extent))])
    return gain


def setup_inputs(seed: int = 0) -> dict:
    streams_of = jax.random.split(jax.random.key(seed), 8)
    return {
        "user_vectors": draw_user_vectors(jax.random.fold_in(streams_of[7], 71), 0),
        "campaigns": draw_campaigns(jax.random.fold_in(streams_of[7], 71), 0),
        "campaign_bids": jnp.clip(jnp.exp(math.log(2.0) - 1.3862944 * jax.random.uniform(streams_of[2], (C,), jnp.float32) ** level_of(streams_of[2], (C,), ((0, 8),), -0.2, 0.2)), 0.5, 2.0),
        "spend_targets": jnp.clip(jnp.exp(math.log(0.02) - 2.30258502 * jax.random.uniform(streams_of[3], (C, SLOTS), jnp.float32) ** level_of(streams_of[3], (C, SLOTS), ((0, 256),), -0.2, 0.2)), 0.002, 0.02),
        "dual_prices": jnp.clip(jnp.exp(math.log(1.5) - 1.60943787 * jax.random.uniform(streams_of[4], (C, SLOTS), jnp.float32) ** level_of(streams_of[4], (C, SLOTS), ((0, 256),), -0.2, 0.2)), 0.3, 1.5),
        "slot_index": touch_ends(jax.random.randint(streams_of[5], (I,), 0, SLOTS), jax.random.fold_in(streams_of[5], 1), 0, SLOTS - 1).astype(jnp.int32),
        "reserve": jnp.clip(12.0 + 8.0 * jax.random.uniform(streams_of[6], (I,), jnp.float32) ** level_of(streams_of[6], (I,), ((0, 32),), -0.2, 0.2), 12.0, 20.0),
    }


def campaign_logits(user_block, slot_block, campaigns, campaign_bids, duals_t):
    affinity = lax.dot_general(user_block, campaigns, (((1,), (1,)), ((), ())), preferred_element_type=jnp.float32)
    return 0.375 * affinity - campaign_bids[None, :] * duals_t[slot_block]

def reference(user_vectors, campaigns, campaign_bids, spend_targets, dual_prices, slot_index, reserve):
    user_rows = user_vectors.shape[0]
    block_rows = min(512, user_rows)
    block_count = user_rows // block_rows
    user_blocks = user_vectors.reshape(block_count, block_rows, E)
    slot_blocks = slot_index.reshape(block_count, block_rows)
    reserve_blocks = reserve.reshape(block_count, block_rows)
    slot_range = jnp.arange(SLOTS, dtype=jnp.int32)
    for step_index in range(ITERS):
        duals_t = dual_prices.T

        def stats_of(pieces):
            user_block, slot_block, reserve_block = pieces
            logits = campaign_logits(user_block, slot_block, campaigns, campaign_bids, duals_t)
            peak = jnp.maximum(lax.optimization_barrier(jnp.max(logits, axis=1)), reserve_block)
            total = jnp.exp(reserve_block - peak) + lax.optimization_barrier(jnp.sum(jnp.exp(logits - peak[:, None]), axis=1))
            return (peak, total)
        row_peak, row_total = lax.map(stats_of, (user_blocks, slot_blocks, reserve_blocks))

        def accumulate(spend_acc, pieces):
            user_block, slot_block, peak_block, total_block = pieces
            logits = campaign_logits(user_block, slot_block, campaigns, campaign_bids, duals_t)
            weights = (jnp.exp(logits - peak_block[:, None]) / total_block[:, None]).astype(jnp.bfloat16)
            slot_hot = (slot_block[:, None] == slot_range[None, :]).astype(jnp.bfloat16)
            term = lax.dot_general(weights, slot_hot, (((0,), (0,)), ((), ())), preferred_element_type=jnp.float32)
            return (spend_acc + term, None)
        spend_acc, unused = lax.scan(accumulate, jnp.zeros((campaigns.shape[0], SLOTS), jnp.float32), (user_blocks, slot_blocks, row_peak, row_total))
        spend_sums = spend_acc * campaign_bids[:, None]
        dual_prices = dual_prices * jnp.sqrt((spend_sums + spend_targets) / (2.0 * spend_targets))
    fill_rate = 1.0 - jnp.exp(reserve_blocks - row_peak) / row_total
    return (dual_prices, fill_rate.reshape(-1))
```

```python
import math

import jax
import jax.numpy as jnp
from jax import lax
from jax.experimental import pallas as pl
from jax.experimental.pallas import tpu as pltpu
from jax.sharding import Mesh, PartitionSpec as P

SLOTS = 96
ITERS = 2
LOG2E = math.log2(math.e)
SCALE = 0.375
TO_LOG2 = SCALE * LOG2E
NX, NZ, NY, NC = 4, 8, 4, 2
LANES = 128
HALF = 512
PACK_ROWS = 80
OWNED = 200
NEAR = NX * OWNED
CAMPS = NC * NEAR
IMPS = NZ * HALF
ROWS = IMPS // LANES
COLS = 256
PIECE = 80
SENT = 4.0
VMEM_LIMIT = 8 * 1024 * 1024
f32, bf16 = jnp.float32, jnp.bfloat16
VMEM = pltpu.VMEM


def shifted(value, axis, size, step):
    return lax.ppermute(value, axis, [(i, (i + step) % size) for i in range(size)])


def in_vmem(kernel, outs, scratch, *operands):
    whole = pl.BlockSpec(memory_space=VMEM)
    return pl.pallas_call(
        kernel,
        in_specs=[whole] * len(operands),
        out_specs=[whole] * len(outs),
        out_shape=[VMEM(shape, dtype) for shape, dtype in outs],
        scratch_shapes=[VMEM(shape, dtype) for shape, dtype in scratch],
        compiler_params=pltpu.CompilerParams(vmem_limit_bytes=VMEM_LIMIT),
    )(*operands)


def one_hot_rows(slot_tile):
    slot_row = slot_tile.astype(f32)[0:1, :]
    return lax.broadcasted_iota(jnp.int32, (SLOTS, slot_row.shape[1]), 0).astype(f32) == slot_row


def folded(value, op):
    parts = [value[r : r + 8] for r in range(0, value.shape[0], 8)]
    total = parts[0]
    for part in parts[1:]:
        total = op(total, part)
    return total


def joined(ref, first, count):
    return jnp.concatenate([ref[pl.ds(first + r, 1), :] for r in range(count)], axis=1)


def stats_kernel(pack_ref, priced_ref, camps_ref, reserve_ref, even_ref, odd_ref, lse_ref, hot_ref, left, right0, right1):
    rights, halves = (right0, right1), (even_ref, odd_ref)
    per_block = COLS // LANES
    for r in range(0, CAMPS, 160):
        rows = slice(r, r + 160)
        high = priced_ref[rows].astype(bf16)
        low = (priced_ref[rows] - high.astype(f32)).astype(bf16)
        left[rows, :LANES] = high + camps_ref[rows, :LANES]
        left[rows, LANES:] = low + camps_ref[rows, LANES:]
    hot_ref[SLOTS:, :] = jnp.zeros((LANES - SLOTS, IMPS), bf16)

    def logits(z, h):
        right, cols = rights[h], slice(h * COLS, (h + 1) * COLS)
        hot = one_hot_rows(pack_ref[z, 64:80, cols]).astype(f32).astype(bf16)
        hot_ref[0:SLOTS, pl.ds(pl.multiple_of(z * HALF + h * COLS, COLS), COLS)] = hot
        right[0:96, :] = hot
        right[96:128, :] = pack_ref[z, 0:32, cols]
        right[128:224, :] = hot
        right[224:256, :] = pack_ref[z, 32:64, cols]
        halves[h][z] = jnp.dot(left[...], right[...], preferred_element_type=f32)

    def top(z, h):
        best = folded(halves[h][z, 0:PIECE], jnp.maximum)
        for r in range(PIECE, CAMPS, PIECE):
            best = jnp.maximum(best, folded(halves[h][z, r : r + PIECE], jnp.maximum))
        return jnp.max(best, axis=0, keepdims=True)

    def weigh(z, h, best):
        first = (z * 2 + h) * per_block
        reserve = joined(reserve_ref, first, per_block)
        peak = jnp.maximum(best * TO_LOG2, reserve)
        total = jnp.zeros((8, COLS), f32)
        for r in range(0, CAMPS, PIECE):
            weights = jnp.exp2(halves[h][z, r : r + PIECE] * TO_LOG2 - peak)
            total = total + folded(weights, jnp.add)
        total = jnp.sum(total, axis=0, keepdims=True) + jnp.exp2(reserve - peak)
        lse = peak + jnp.log2(total)
        for r in range(per_block):
            lse_ref[pl.ds(first + r, 1), :] = lse[:, r * LANES : (r + 1) * LANES]

    def both(z, best0):
        logits(z, 1)
        weigh(z, 0, best0)
        best1 = top(z, 1)
        following = jnp.minimum(z + 1, NZ - 1)
        logits(following, 0)
        weigh(z, 1, best1)
        return top(following, 0)

    logits(0, 0)
    lax.fori_loop(0, NZ, both, top(0, 0))


def local_stats(pack, priced, camps, reserve):
    return in_vmem(
        stats_kernel,
        [((NZ, CAMPS, COLS), f32)] * 2 + [((ROWS, LANES), f32), ((LANES, IMPS), bf16)],
        [((CAMPS, 2 * LANES), bf16), ((2 * LANES, COLS), bf16), ((2 * LANES, COLS), bf16)],
        pack, priced, camps, reserve,
    )


def merged(pieces):
    top = pieces[0]
    for piece in pieces[1:]:
        top = jnp.maximum(top, piece)
    return top + jnp.log2(sum(jnp.exp2(piece - top) for piece in pieces))


def spent(first, even_ref, odd_ref, hot_ref, lse_ref, spend_ref, weights0, weights1):
    def columns(z):
        return pl.ds(pl.multiple_of(z * HALF, HALF), HALF)

    def weigh(z, weights):
        per_block = COLS // LANES
        for h, logits_ref in enumerate((even_ref, odd_ref)):
            lse = joined(lse_ref, (z * 2 + h) * per_block, per_block)
            for r in range(0, NEAR, PIECE):
                logits = logits_ref[z, first + r : first + r + PIECE]
                weights[r : r + PIECE, h * COLS : (h + 1) * COLS] = jnp.exp2(
                    logits * TO_LOG2 - lse
                ).astype(bf16)

    def gather(z, weights):
        spend_ref[...] += lax.dot_general(
            weights[...], hot_ref[:, columns(z)], (((1,), (1,)), ((), ())), preferred_element_type=f32
        )

    def both(k, carry):
        gather(2 * k, weights0)
        weigh(2 * k + 1, weights1)
        gather(2 * k + 1, weights1)
        weigh(jnp.minimum(2 * k + 2, NZ - 1), weights0)
        return carry

    spend_ref[...] = jnp.zeros(spend_ref.shape, f32)
    weigh(0, weights0)
    lax.fori_loop(0, NZ // 2, both, 0)


def far_kernel(even_ref, odd_ref, hot_ref, parts_ref, far_ref, lse_ref, weights0, weights1):
    lse_ref[...] = merged([parts_ref[k] for k in range(NZ)])
    spent(NEAR, even_ref, odd_ref, hot_ref, lse_ref, far_ref, weights0, weights1)


def near_kernel(*refs):
    spent(0, *refs)


WEIGHTS = [((NEAR, HALF), bf16)] * 2


def far_spend(even, odd, hot, parts):
    return in_vmem(
        far_kernel, [((NEAR, LANES), f32), ((ROWS, LANES), f32)], WEIGHTS, even, odd, hot, parts
    )


def near_spend(even, odd, hot, lse):
    return in_vmem(near_kernel, [((NEAR, LANES), f32)], WEIGHTS, even, odd, hot, lse)[0]


def prep_kernel(*refs):
    sources, (packs_ref, state_ref), landed, square, sems = refs[:4], refs[4:6], refs[6:10], *refs[10:]
    copies = [
        pltpu.make_async_copy(source, target, sems.at[k])
        for k, (source, target) in enumerate(zip(sources, landed))
    ]
    for copy in copies:
        copy.start()
    for copy in copies:
        copy.wait()
    users_ref, slots_ref, duals_ref, targets_ref = landed
    near = lax.axis_index("core") == 0
    users = jnp.where(near, users_ref[:, :HALF].astype(f32), users_ref[:, HALF:].astype(f32))
    half = HALF // LANES
    slots = jnp.where(near, slots_ref[:half], slots_ref[half:]).astype(f32)
    slots = jnp.concatenate([slots[r : r + 1] for r in range(half)], axis=1)
    tail = jnp.broadcast_to(slots, (PACK_ROWS - 64, HALF)).astype(bf16)
    for k in range(NZ):
        packs_ref[k, 0:64, :] = users.astype(bf16)
        packs_ref[k, 64:80, :] = tail
    square[...] = jnp.zeros(square.shape, f32)
    square[0:SLOTS, 0:OWNED] = duals_ref[...]
    state_ref[:, :LANES] = square[...].T[:OWNED]
    square[0:SLOTS, 0:OWNED] = 0.5 / targets_ref[...]
    state_ref[:, LANES:] = square[...].T[:OWNED]


def prepared(users, slots, duals, targets):
    operands = users.T, slots.reshape(-1, LANES), duals.T, targets.T
    operands = [pltpu.with_memory_space_constraint(a, pltpu.HBM) for a in operands]
    return pl.pallas_call(
        prep_kernel,
        in_specs=[pl.BlockSpec(memory_space=pltpu.HBM)] * 4,
        out_specs=[pl.BlockSpec(memory_space=VMEM)] * 2,
        out_shape=[VMEM((NZ, PACK_ROWS, HALF), bf16), VMEM((OWNED, 2 * LANES), f32)],
        scratch_shapes=[VMEM(a.shape, a.dtype) for a in operands]
        + [VMEM((LANES, 2 * LANES), f32), pltpu.SemaphoreType.DMA((4,))],
        compiler_params=pltpu.CompilerParams(vmem_limit_bytes=VMEM_LIMIT),
    )(*operands)


def near_rows(array, x, z):
    starts = [((x + NX - s) % NX) * (NZ * OWNED) + z * OWNED for s in range(NX)]
    return jnp.concatenate([lax.dynamic_slice_in_dim(array, at, OWNED, 0) for at in starts])


def both_cores(near):
    return jnp.concatenate([near, shifted(near, "core", NC, 1)])


def over_x(owned):
    return jnp.concatenate([owned] + [shifted(owned, "x", NX, s) for s in range(1, NX)])


def shards(user_vectors, campaigns, campaign_bids, spend_targets, dual_prices, slot_index, reserve):
    x, z, y, core = (lax.axis_index(a) for a in ("x", "z", "y", "core"))
    pack, state = prepared(user_vectors, slot_index, dual_prices, spend_targets)
    pack = lax.all_to_all(pack, "z", 0, 0, tiled=True)
    state = over_x(state)
    z_late, state = lax.optimization_barrier((z, state))
    bids = near_rows(campaign_bids, x, z_late)[:, None]
    priced, rates = state[:, :LANES] * (bids * (-1.0 / SCALE)), state[:, LANES:] * bids

    camps = both_cores(near_rows(campaigns, x, z_late))
    blank = jnp.zeros((CAMPS, SLOTS), bf16)
    camps = jnp.concatenate([blank, camps[:, :32], blank, camps[:, 32:]], axis=1)

    own_reserve = (
        lax.dynamic_slice_in_dim(reserve, core * HALF, HALF, 0) * LOG2E
    ).reshape(1, HALF // LANES, LANES)
    at_home = (lax.broadcasted_iota(jnp.int32, (NZ, 1, 1), 0) == z) & (y == 0)
    wide_reserve = jnp.where(at_home, own_reserve, -1e30).reshape(ROWS, LANES)

    gain = 1.0
    for step in range(ITERS):
        even, odd, lse, hot = local_stats(pack, both_cores(priced), camps, wide_reserve)
        lse = merged([lse] + [shifted(lse, "y", NY, s) for s in range(1, NY)])
        parts = lax.all_to_all(
            jnp.broadcast_to(lse[None], (NZ, ROWS, LANES)), "z", 0, 0, tiled=True
        )
        far, lse = far_spend(even, odd, hot, parts)
        far = shifted(far, "core", NC, 1)
        spend = near_spend(even, odd, hot, lse) + far
        sent = (spend * SENT).astype(jnp.float16)
        if step + 1 < ITERS:
            for s in range(1, NX):
                spend = spend + jnp.roll(shifted(sent, "x", NX, s), s * OWNED, 0).astype(f32) * (1.0 / SENT)
            factor = jnp.sqrt(0.5 + spend * rates)
            priced = priced * factor
            gain = factor[:OWNED]
        else:
            own = spend[:OWNED]
            for s in range(1, NX):
                block = shifted(sent[s * OWNED : (s + 1) * OWNED], "x", NX, -s)
                own = own + block.astype(f32) * (1.0 / SENT)
            gain = gain * jnp.sqrt(0.5 + own * rates[:OWNED])

    home = lax.dynamic_slice_in_dim(lse.reshape(NZ, HALF), z, 1, 0).reshape(HALF)
    far = shifted(home, "core", NC, 1)
    row_lse = jnp.where(core == 0, jnp.concatenate([home, far]), jnp.concatenate([far, home]))
    fill_rate = 1.0 - jnp.exp2(reserve * LOG2E - row_lse)
    return dual_prices * gain[:, :SLOTS], fill_rate


def solution(mesh):
    split = Mesh(mesh.devices.reshape(NX, NZ, NY, NC), ("x", "z", "y", "core"))
    wide, narrow = ("x", "z"), ("y", "core")
    placed = (
        P(wide, None),
        P(narrow, None),
        P(narrow),
        P(narrow + wide, None),
        P(narrow + wide, None),
        P(wide),
        P(wide),
    )
    return jax.shard_map(
        shards,
        mesh=split,
        in_specs=placed,
        out_specs=(P(narrow + wide, None), P(wide)),
        check_vma=False,
    )
```

```python
import math

import jax
import jax.numpy as jnp
from jax import lax
from jax.experimental import pallas as pl
from jax.experimental.pallas import tpu as pltpu
from jax.sharding import Mesh, PartitionSpec as P

SLOTS = 96
ITERS = 2
LOG2E = math.log2(math.e)
SCALE = 0.375
TO_LOG2 = SCALE * LOG2E
NX, NZ, NY, NC = 4, 8, 4, 2
LANES = 128
HALF = 512
PACK_ROWS = 80
OWNED = 200
NEAR = NX * OWNED
CAMPS = NC * NEAR
IMPS = NZ * HALF
ROWS = IMPS // LANES
COLS = 256
PIECE = 80
SENT = 4.0
VMEM_LIMIT = 8 * 1024 * 1024
f32, bf16 = jnp.float32, jnp.bfloat16
VMEM = pltpu.VMEM


def shifted(value, axis, size, step):
    return lax.ppermute(value, axis, [(i, (i + step) % size) for i in range(size)])


def in_vmem(kernel, outs, scratch, *operands):
    whole = pl.BlockSpec(memory_space=VMEM)
    return pl.pallas_call(
        kernel,
        in_specs=[whole] * len(operands),
        out_specs=[whole] * len(outs),
        out_shape=[VMEM(shape, dtype) for shape, dtype in outs],
        scratch_shapes=[VMEM(shape, dtype) for shape, dtype in scratch],
        compiler_params=pltpu.CompilerParams(vmem_limit_bytes=VMEM_LIMIT),
    )(*operands)


def one_hot_rows(slot_tile):
    slot_row = slot_tile.astype(f32)[0:1, :]
    return lax.broadcasted_iota(jnp.int32, (SLOTS, slot_row.shape[1]), 0).astype(f32) == slot_row


def folded(value, op):
    parts = [value[r : r + 8] for r in range(0, value.shape[0], 8)]
    total = parts[0]
    for part in parts[1:]:
        total = op(total, part)
    return total


def joined(ref, first, count):
    return jnp.concatenate([ref[pl.ds(first + r, 1), :] for r in range(count)], axis=1)


def stats_kernel(pack_ref, priced_ref, camps_ref, reserve_ref, even_ref, odd_ref, lse_ref, hot_ref, left, right0, right1):
    rights, halves = (right0, right1), (even_ref, odd_ref)
    per_block = COLS // LANES
    for r in range(0, CAMPS, 160):
        rows = slice(r, r + 160)
        high = priced_ref[rows].astype(bf16)
        low = (priced_ref[rows] - high.astype(f32)).astype(bf16)
        left[rows, :LANES] = high + camps_ref[rows, :LANES]
        left[rows, LANES:] = low + camps_ref[rows, LANES:]
    hot_ref[SLOTS:, :] = jnp.zeros((LANES - SLOTS, IMPS), bf16)

    def logits(z, h):
        right, cols = rights[h], slice(h * COLS, (h + 1) * COLS)
        hot = one_hot_rows(pack_ref[z, 64:80, cols]).astype(f32).astype(bf16)
        hot_ref[0:SLOTS, pl.ds(pl.multiple_of(z * HALF + h * COLS, COLS), COLS)] = hot
        right[0:96, :] = hot
        right[96:128, :] = pack_ref[z, 0:32, cols]
        right[128:224, :] = hot
        right[224:256, :] = pack_ref[z, 32:64, cols]
        halves[h][z] = jnp.dot(left[...], right[...], preferred_element_type=f32)

    def top(z, h):
        best = folded(halves[h][z, 0:PIECE], jnp.maximum)
        for r in range(PIECE, CAMPS, PIECE):
            best = jnp.maximum(best, folded(halves[h][z, r : r + PIECE], jnp.maximum))
        return jnp.max(best, axis=0, keepdims=True)

    def weigh(z, h, best):
        first = (z * 2 + h) * per_block
        reserve = joined(reserve_ref, first, per_block)
        peak = jnp.maximum(best * TO_LOG2, reserve)
        total = jnp.zeros((8, COLS), f32)
        for r in range(0, CAMPS, PIECE):
            weights = jnp.exp2(halves[h][z, r : r + PIECE] * TO_LOG2 - peak)
            total = total + folded(weights, jnp.add)
        total = jnp.sum(total, axis=0, keepdims=True) + jnp.exp2(reserve - peak)
        lse = peak + jnp.log2(total)
        for r in range(per_block):
            lse_ref[pl.ds(first + r, 1), :] = lse[:, r * LANES : (r + 1) * LANES]

    def both(z, best0):
        logits(z, 1)
        weigh(z, 0, best0)
        best1 = top(z, 1)
        if z + 1 < NZ:
            logits(z + 1, 0)
        weigh(z, 1, best1)
        return top(z + 1, 0) if z + 1 < NZ else None

    logits(0, 0)
    best = top(0, 0)
    for z in range(NZ):
        best = both(z, best)


def local_stats(pack, priced, camps, reserve):
    return in_vmem(
        stats_kernel,
        [((NZ, CAMPS, COLS), f32)] * 2 + [((ROWS, LANES), f32), ((LANES, IMPS), bf16)],
        [((CAMPS, 2 * LANES), bf16), ((2 * LANES, COLS), bf16), ((2 * LANES, COLS), bf16)],
        pack, priced, camps, reserve,
    )


def merged(pieces):
    top = pieces[0]
    for piece in pieces[1:]:
        top = jnp.maximum(top, piece)
    return top + jnp.log2(sum(jnp.exp2(piece - top) for piece in pieces))


def spent(first, even_ref, odd_ref, hot_ref, lse_ref, spend_ref, weights0, weights1):
    def columns(z):
        return pl.ds(pl.multiple_of(z * HALF, HALF), HALF)

    def weigh(z, weights):
        per_block = COLS // LANES
        for h, logits_ref in enumerate((even_ref, odd_ref)):
            lse = joined(lse_ref, (z * 2 + h) * per_block, per_block)
            for r in range(0, NEAR, PIECE):
                logits = logits_ref[z, first + r : first + r + PIECE]
                weights[r : r + PIECE, h * COLS : (h + 1) * COLS] = jnp.exp2(
                    logits * TO_LOG2 - lse
                ).astype(bf16)

    def gather(z, weights):
        spend_ref[...] += lax.dot_general(
            weights[...], hot_ref[:, columns(z)], (((1,), (1,)), ((), ())), preferred_element_type=f32
        )

    def both(k, carry):
        gather(2 * k, weights0)
        weigh(2 * k + 1, weights1)
        gather(2 * k + 1, weights1)
        weigh(jnp.minimum(2 * k + 2, NZ - 1), weights0)
        return carry

    spend_ref[...] = jnp.zeros(spend_ref.shape, f32)
    weigh(0, weights0)
    lax.fori_loop(0, NZ // 2, both, 0)


def far_kernel(even_ref, odd_ref, hot_ref, parts_ref, far_ref, lse_ref, weights0, weights1):
    lse_ref[...] = merged([parts_ref[k] for k in range(NZ)])
    spent(NEAR, even_ref, odd_ref, hot_ref, lse_ref, far_ref, weights0, weights1)


def near_kernel(*refs):
    spent(0, *refs)


def joint_kernel(even_ref, odd_ref, hot_ref, parts_ref, far_ref, near_ref, lse_ref, *weights):
    lse_ref[...] = merged([parts_ref[k] for k in range(NZ)])
    spent(NEAR, even_ref, odd_ref, hot_ref, lse_ref, far_ref, *weights)
    spent(0, even_ref, odd_ref, hot_ref, lse_ref, near_ref, *weights)


WEIGHTS = [((NEAR, HALF), bf16)] * 2


def far_spend(even, odd, hot, parts):
    return in_vmem(
        far_kernel, [((NEAR, LANES), f32), ((ROWS, LANES), f32)], WEIGHTS, even, odd, hot, parts
    )


def joint_spend(even, odd, hot, parts):
    return in_vmem(
        joint_kernel,
        [((NEAR, LANES), f32)] * 2 + [((ROWS, LANES), f32)],
        WEIGHTS,
        even, odd, hot, parts,
    )


def near_spend(even, odd, hot, lse):
    return in_vmem(near_kernel, [((NEAR, LANES), f32)], WEIGHTS, even, odd, hot, lse)[0]


def prep_kernel(*refs):
    sources, (packs_ref, state_ref), landed, square, sems = refs[:4], refs[4:6], refs[6:10], *refs[10:]
    copies = [
        pltpu.make_async_copy(source, target, sems.at[k])
        for k, (source, target) in enumerate(zip(sources, landed))
    ]
    for copy in copies:
        copy.start()
    for copy in copies:
        copy.wait()
    users_ref, slots_ref, duals_ref, targets_ref = landed
    near = lax.axis_index("core") == 0
    users = jnp.where(near, users_ref[:, :HALF].astype(f32), users_ref[:, HALF:].astype(f32))
    half = HALF // LANES
    slots = jnp.where(near, slots_ref[:half], slots_ref[half:]).astype(f32)
    slots = jnp.concatenate([slots[r : r + 1] for r in range(half)], axis=1)
    tail = jnp.broadcast_to(slots, (PACK_ROWS - 64, HALF)).astype(bf16)
    for k in range(NZ):
        packs_ref[k, 0:64, :] = users.astype(bf16)
        packs_ref[k, 64:80, :] = tail
    square[...] = jnp.zeros(square.shape, f32)
    square[0:SLOTS, 0:OWNED] = duals_ref[...]
    state_ref[:, :LANES] = square[...].T[:OWNED]
    square[0:SLOTS, 0:OWNED] = 0.5 / targets_ref[...]
    state_ref[:, LANES:] = square[...].T[:OWNED]


def prepared(users, slots, duals, targets):
    operands = users.T, slots.reshape(-1, LANES), duals.T, targets.T
    operands = [pltpu.with_memory_space_constraint(a, pltpu.HBM) for a in operands]
    return pl.pallas_call(
        prep_kernel,
        in_specs=[pl.BlockSpec(memory_space=pltpu.HBM)] * 4,
        out_specs=[pl.BlockSpec(memory_space=VMEM)] * 2,
        out_shape=[VMEM((NZ, PACK_ROWS, HALF), bf16), VMEM((OWNED, 2 * LANES), f32)],
        scratch_shapes=[VMEM(a.shape, a.dtype) for a in operands]
        + [VMEM((LANES, 2 * LANES), f32), pltpu.SemaphoreType.DMA((4,))],
        compiler_params=pltpu.CompilerParams(vmem_limit_bytes=VMEM_LIMIT),
    )(*operands)


def near_rows(array, x, z):
    starts = [((x + NX - s) % NX) * (NZ * OWNED) + z * OWNED for s in range(NX)]
    return jnp.concatenate([lax.dynamic_slice_in_dim(array, at, OWNED, 0) for at in starts])


def both_cores(near):
    return jnp.concatenate([near, shifted(near, "core", NC, 1)])


def over_x(owned):
    return jnp.concatenate([owned] + [shifted(owned, "x", NX, s) for s in range(1, NX)])


def shards(user_vectors, campaigns, campaign_bids, spend_targets, dual_prices, slot_index, reserve):
    x, z, y, core = (lax.axis_index(a) for a in ("x", "z", "y", "core"))
    pack, state = prepared(user_vectors, slot_index, dual_prices, spend_targets)
    pack = lax.all_to_all(pack, "z", 0, 0, tiled=True)
    state = over_x(state)
    z_late, state = lax.optimization_barrier((z, state))
    bids = near_rows(campaign_bids, x, z_late)[:, None]
    priced, rates = state[:, :LANES] * (bids * (-1.0 / SCALE)), state[:, LANES:] * bids

    camps = both_cores(near_rows(campaigns, x, z_late))
    blank = jnp.zeros((CAMPS, SLOTS), bf16)
    camps = jnp.concatenate([blank, camps[:, :32], blank, camps[:, 32:]], axis=1)

    own_reserve = (
        lax.dynamic_slice_in_dim(reserve, core * HALF, HALF, 0) * LOG2E
    ).reshape(1, HALF // LANES, LANES)
    at_home = (lax.broadcasted_iota(jnp.int32, (NZ, 1, 1), 0) == z) & (y == 0)
    wide_reserve = jnp.where(at_home, own_reserve, -1e30).reshape(ROWS, LANES)

    gain = 1.0
    for step in range(ITERS):
        even, odd, lse, hot = local_stats(pack, both_cores(priced), camps, wide_reserve)
        lse = merged([lse] + [shifted(lse, "y", NY, s) for s in range(1, NY)])
        parts = lax.all_to_all(
            jnp.broadcast_to(lse[None], (NZ, ROWS, LANES)), "z", 0, 0, tiled=True
        )
        if step + 1 < ITERS:
            far, lse = far_spend(even, odd, hot, parts)
            far = shifted(far, "core", NC, 1)
            near = near_spend(even, odd, hot, lse)
        else:
            far, near, lse = joint_spend(even, odd, hot, parts)
            far = shifted(far, "core", NC, 1)
        spend = near + far
        sent = (spend * SENT).astype(jnp.float16)
        if step + 1 < ITERS:
            for s in range(1, NX):
                spend = spend + jnp.roll(shifted(sent, "x", NX, s), s * OWNED, 0).astype(f32) * (1.0 / SENT)
            factor = jnp.sqrt(0.5 + spend * rates)
            priced = priced * factor
            gain = factor[:OWNED]
        else:
            own = spend[:OWNED]
            for s in range(1, NX):
                block = shifted(sent[s * OWNED : (s + 1) * OWNED], "x", NX, -s)
                own = own + block.astype(f32) * (1.0 / SENT)
            gain = gain * jnp.sqrt(0.5 + own * rates[:OWNED])

    home = lax.dynamic_slice_in_dim(lse.reshape(NZ, HALF), z, 1, 0).reshape(HALF)
    far = shifted(home, "core", NC, 1)
    row_lse = jnp.where(core == 0, jnp.concatenate([home, far]), jnp.concatenate([far, home]))
    fill_rate = 1.0 - jnp.exp2(reserve * LOG2E - row_lse)
    return dual_prices * gain[:, :SLOTS], fill_rate


def solution(mesh):
    split = Mesh(mesh.devices.reshape(NX, NZ, NY, NC), ("x", "z", "y", "core"))
    wide, narrow = ("x", "z"), ("y", "core")
    placed = (
        P(wide, None),
        P(narrow, None),
        P(narrow),
        P(narrow + wide, None),
        P(narrow + wide, None),
        P(wide),
        P(wide),
    )
    return jax.shard_map(
        shards,
        mesh=split,
        in_specs=placed,
        out_specs=(P(narrow + wide, None), P(wide)),
        check_vma=False,
    )
```

```python
import math

import jax
import jax.numpy as jnp
from jax import lax
from jax.experimental import pallas as pl
from jax.experimental.pallas import tpu as pltpu
from jax.sharding import Mesh, PartitionSpec as P

SLOTS = 96
ITERS = 2
LOG2E = math.log2(math.e)
SCALE = 0.375
TO_LOG2 = SCALE * LOG2E
NX, NZ, NY, NC = 4, 8, 4, 2
LANES = 128
HALF = 512
PACK_ROWS = 80
OWNED = 200
NEAR = NX * OWNED
CAMPS = NC * NEAR
IMPS = NZ * HALF
ROWS = IMPS // LANES
COLS = 256
PIECE = 80
SENT = 4.0
VMEM_LIMIT = 8 * 1024 * 1024
f32, bf16 = jnp.float32, jnp.bfloat16
VMEM = pltpu.VMEM


def shifted(value, axis, size, step):
    return lax.ppermute(value, axis, [(i, (i + step) % size) for i in range(size)])


def in_vmem(kernel, outs, scratch, *operands):
    whole = pl.BlockSpec(memory_space=VMEM)
    return pl.pallas_call(
        kernel,
        in_specs=[whole] * len(operands),
        out_specs=[whole] * len(outs),
        out_shape=[VMEM(shape, dtype) for shape, dtype in outs],
        scratch_shapes=[VMEM(shape, dtype) for shape, dtype in scratch],
        compiler_params=pltpu.CompilerParams(vmem_limit_bytes=VMEM_LIMIT),
    )(*operands)


def one_hot_rows(slot_tile):
    slot_row = slot_tile.astype(f32)[0:1, :]
    return lax.broadcasted_iota(jnp.int32, (SLOTS, slot_row.shape[1]), 0).astype(f32) == slot_row


def folded(value, op):
    parts = [value[r : r + 8] for r in range(0, value.shape[0], 8)]
    total = parts[0]
    for part in parts[1:]:
        total = op(total, part)
    return total


def joined(ref, first, count):
    return jnp.concatenate([ref[pl.ds(first + r, 1), :] for r in range(count)], axis=1)


def stats_kernel(pack_ref, priced_ref, camps_ref, reserve_ref, even_ref, odd_ref, lse_ref, hot_ref, left, right0, right1):
    rights, halves = (right0, right1), (even_ref, odd_ref)
    per_block = COLS // LANES
    for r in range(0, CAMPS, 160):
        rows = slice(r, r + 160)
        high = priced_ref[rows].astype(bf16)
        low = (priced_ref[rows] - high.astype(f32)).astype(bf16)
        left[rows, :LANES] = high + camps_ref[rows, :LANES]
        left[rows, LANES:] = low + camps_ref[rows, LANES:]
    hot_ref[SLOTS:, :] = jnp.zeros((LANES - SLOTS, IMPS), bf16)

    def logits(z, h):
        right, cols = rights[h], slice(h * COLS, (h + 1) * COLS)
        hot = one_hot_rows(pack_ref[z, 64:80, cols]).astype(f32).astype(bf16)
        hot_ref[0:SLOTS, pl.ds(pl.multiple_of(z * HALF + h * COLS, COLS), COLS)] = hot
        right[0:96, :] = hot
        right[96:128, :] = pack_ref[z, 0:32, cols]
        right[128:224, :] = hot
        right[224:256, :] = pack_ref[z, 32:64, cols]
        halves[h][z] = jnp.dot(left[...], right[...], preferred_element_type=f32)

    def top(z, h):
        best = folded(halves[h][z, 0:PIECE], jnp.maximum)
        for r in range(PIECE, CAMPS, PIECE):
            best = jnp.maximum(best, folded(halves[h][z, r : r + PIECE], jnp.maximum))
        return jnp.max(best, axis=0, keepdims=True)

    def weigh(z, h, best):
        first = (z * 2 + h) * per_block
        reserve = joined(reserve_ref, first, per_block)
        peak = jnp.maximum(best * TO_LOG2, reserve)
        total = jnp.zeros((8, COLS), f32)
        for r in range(0, CAMPS, PIECE):
            weights = jnp.exp2(halves[h][z, r : r + PIECE] * TO_LOG2 - peak)
            total = total + folded(weights, jnp.add)
        total = jnp.sum(total, axis=0, keepdims=True) + jnp.exp2(reserve - peak)
        lse = peak + jnp.log2(total)
        for r in range(per_block):
            lse_ref[pl.ds(first + r, 1), :] = lse[:, r * LANES : (r + 1) * LANES]

    def both(z, best0):
        logits(z, 1)
        weigh(z, 0, best0)
        best1 = top(z, 1)
        if z + 1 < NZ:
            logits(z + 1, 0)
        weigh(z, 1, best1)
        return top(z + 1, 0) if z + 1 < NZ else None

    logits(0, 0)
    best = top(0, 0)
    for z in range(NZ):
        best = both(z, best)


def local_stats(pack, priced, camps, reserve):
    return in_vmem(
        stats_kernel,
        [((NZ, CAMPS, COLS), f32)] * 2 + [((ROWS, LANES), f32), ((LANES, IMPS), bf16)],
        [((CAMPS, 2 * LANES), bf16), ((2 * LANES, COLS), bf16), ((2 * LANES, COLS), bf16)],
        pack, priced, camps, reserve,
    )


def merged(pieces):
    top = pieces[0]
    for piece in pieces[1:]:
        top = jnp.maximum(top, piece)
    return top + jnp.log2(sum(jnp.exp2(piece - top) for piece in pieces))


def spent(first, even_ref, odd_ref, hot_ref, lse_ref, spend_ref, weights0, weights1):
    def columns(z):
        return pl.ds(pl.multiple_of(z * HALF, HALF), HALF)

    def weigh(z, weights):
        per_block = COLS // LANES
        for h, logits_ref in enumerate((even_ref, odd_ref)):
            lse = joined(lse_ref, (z * 2 + h) * per_block, per_block)
            for r in range(0, NEAR, PIECE):
                logits = logits_ref[z, first + r : first + r + PIECE]
                weights[r : r + PIECE, h * COLS : (h + 1) * COLS] = jnp.exp2(
                    logits * TO_LOG2 - lse
                ).astype(bf16)

    def gather(z, weights):
        spend_ref[...] += lax.dot_general(
            weights[...], hot_ref[:, columns(z)], (((1,), (1,)), ((), ())), preferred_element_type=f32
        )

    def both(k, carry):
        gather(2 * k, weights0)
        weigh(2 * k + 1, weights1)
        gather(2 * k + 1, weights1)
        weigh(jnp.minimum(2 * k + 2, NZ - 1), weights0)
        return carry

    spend_ref[...] = jnp.zeros(spend_ref.shape, f32)
    weigh(0, weights0)
    lax.fori_loop(0, NZ // 2, both, 0)


def far_kernel(even_ref, odd_ref, hot_ref, parts_ref, far_ref, lse_ref, weights0, weights1):
    lse_ref[...] = merged([parts_ref[k] for k in range(NZ)])
    spent(NEAR, even_ref, odd_ref, hot_ref, lse_ref, far_ref, weights0, weights1)


def near_kernel(*refs):
    spent(0, *refs)


def joint_kernel(even_ref, odd_ref, hot_ref, parts_ref, far_ref, near_ref, lse_ref, *weights):
    lse_ref[...] = merged([parts_ref[k] for k in range(NZ)])
    spent(NEAR, even_ref, odd_ref, hot_ref, lse_ref, far_ref, *weights)
    spent(0, even_ref, odd_ref, hot_ref, lse_ref, near_ref, *weights)


WEIGHTS = [((NEAR, HALF), bf16)] * 2


def far_spend(even, odd, hot, parts):
    return in_vmem(
        far_kernel, [((NEAR, LANES), f32), ((ROWS, LANES), f32)], WEIGHTS, even, odd, hot, parts
    )


def joint_spend(even, odd, hot, parts):
    return in_vmem(
        joint_kernel,
        [((NEAR, LANES), f32)] * 2 + [((ROWS, LANES), f32)],
        WEIGHTS,
        even, odd, hot, parts,
    )


def near_spend(even, odd, hot, lse):
    return in_vmem(near_kernel, [((NEAR, LANES), f32)], WEIGHTS, even, odd, hot, lse)[0]


def landed(sources, targets, sems):
    copies = [
        pltpu.make_async_copy(source, target, sems.at[k])
        for k, (source, target) in enumerate(zip(sources, targets))
    ]
    for copy in copies:
        copy.start()
    for copy in copies:
        copy.wait()


def pack_kernel(users_hbm, slots_hbm, packs_ref, users_ref, slots_ref, sems):
    landed((users_hbm, slots_hbm), (users_ref, slots_ref), sems)
    near = lax.axis_index("core") == 0
    users = jnp.where(near, users_ref[:, :HALF].astype(f32), users_ref[:, HALF:].astype(f32))
    half = HALF // LANES
    slots = jnp.where(near, slots_ref[:half], slots_ref[half:]).astype(f32)
    slots = jnp.concatenate([slots[r : r + 1] for r in range(half)], axis=1)
    tail = jnp.broadcast_to(slots, (PACK_ROWS - 64, HALF)).astype(bf16)
    for k in range(NZ):
        packs_ref[k, 0:64, :] = users.astype(bf16)
        packs_ref[k, 64:80, :] = tail


def state_kernel(duals_hbm, targets_hbm, after, state_ref, duals_ref, targets_ref, square, sems):
    landed((duals_hbm, targets_hbm), (duals_ref, targets_ref), sems)
    square[...] = jnp.zeros(square.shape, f32)
    square[0:SLOTS, 0:OWNED] = duals_ref[...]
    state_ref[:, :LANES] = square[...].T[:OWNED]
    square[0:SLOTS, 0:OWNED] = 0.5 / targets_ref[...]
    state_ref[:, LANES:] = square[...].T[:OWNED]


def from_hbm(kernel, out, scratch, operands, *after):
    operands = [pltpu.with_memory_space_constraint(a, pltpu.HBM) for a in operands]
    hbm, vmem = pl.BlockSpec(memory_space=pltpu.HBM), pl.BlockSpec(memory_space=VMEM)
    return pl.pallas_call(
        kernel,
        in_specs=[hbm] * len(operands) + [vmem] * len(after),
        out_specs=vmem,
        out_shape=VMEM(*out),
        scratch_shapes=[VMEM(a.shape, a.dtype) for a in operands]
        + scratch
        + [pltpu.SemaphoreType.DMA((len(operands),))],
        compiler_params=pltpu.CompilerParams(vmem_limit_bytes=VMEM_LIMIT),
    )(*operands, *after)


def near_rows(array, x, z):
    starts = [((x + NX - s) % NX) * (NZ * OWNED) + z * OWNED for s in range(NX)]
    return jnp.concatenate([lax.dynamic_slice_in_dim(array, at, OWNED, 0) for at in starts])


def both_cores(near):
    return jnp.concatenate([near, shifted(near, "core", NC, 1)])


def over_x(owned):
    return jnp.concatenate([owned] + [shifted(owned, "x", NX, s) for s in range(1, NX)])


def shards(user_vectors, campaigns, campaign_bids, spend_targets, dual_prices, slot_index, reserve):
    x, z, y, core = (lax.axis_index(a) for a in ("x", "z", "y", "core"))
    pack = from_hbm(
        pack_kernel,
        ((NZ, PACK_ROWS, HALF), bf16),
        [],
        (user_vectors.T, slot_index.reshape(-1, LANES)),
    )
    token = shifted(pack[0, 64:80, :LANES], "core", NC, 1)
    pack = lax.all_to_all(pack, "z", 0, 0, tiled=True)
    state = over_x(
        from_hbm(
            state_kernel,
            ((OWNED, 2 * LANES), f32),
            [VMEM((LANES, 2 * LANES), f32)],
            (dual_prices.T, spend_targets.T),
            token,
        )
    )
    z_late, state = lax.optimization_barrier((z, state))
    camps = both_cores(near_rows(campaigns, x, z_late))
    blank = jnp.zeros((CAMPS, SLOTS), bf16)
    camps = jnp.concatenate([blank, camps[:, :32], blank, camps[:, 32:]], axis=1)
    bids = near_rows(campaign_bids, x, z_late)[:, None]
    priced, rates = state[:, :LANES] * (bids * (-1.0 / SCALE)), state[:, LANES:] * bids

    own_reserve = (
        lax.dynamic_slice_in_dim(reserve, core * HALF, HALF, 0) * LOG2E
    ).reshape(1, HALF // LANES, LANES)
    at_home = (lax.broadcasted_iota(jnp.int32, (NZ, 1, 1), 0) == z) & (y == 0)
    wide_reserve = jnp.where(at_home, own_reserve, -1e30).reshape(ROWS, LANES)

    gain = 1.0
    for step in range(ITERS):
        even, odd, lse, hot = local_stats(pack, both_cores(priced), camps, wide_reserve)
        lse = merged([lse] + [shifted(lse, "y", NY, s) for s in range(1, NY)])
        parts = lax.all_to_all(
            jnp.broadcast_to(lse[None], (NZ, ROWS, LANES)), "z", 0, 0, tiled=True
        )
        if step + 1 < ITERS:
            far, lse = far_spend(even, odd, hot, parts)
            far = shifted(far, "core", NC, 1)
            near = near_spend(even, odd, hot, lse)
        else:
            far, near, lse = joint_spend(even, odd, hot, parts)
            far = shifted(far, "core", NC, 1)
        spend = near + far
        sent = (spend * SENT).astype(jnp.float16)
        if step + 1 < ITERS:
            for s in range(1, NX):
                spend = spend + jnp.roll(shifted(sent, "x", NX, s), s * OWNED, 0).astype(f32) * (1.0 / SENT)
            factor = jnp.sqrt(0.5 + spend * rates)
            priced = priced * factor
            gain = factor[:OWNED]
        else:
            own = spend[:OWNED]
            for s in range(1, NX):
                block = shifted(sent[s * OWNED : (s + 1) * OWNED], "x", NX, -s)
                own = own + block.astype(f32) * (1.0 / SENT)
            gain = gain * jnp.sqrt(0.5 + own * rates[:OWNED])

    home = lax.dynamic_slice_in_dim(lse.reshape(NZ, HALF), z, 1, 0).reshape(HALF)
    far = shifted(home, "core", NC, 1)
    row_lse = jnp.where(core == 0, jnp.concatenate([home, far]), jnp.concatenate([far, home]))
    fill_rate = 1.0 - jnp.exp2(reserve * LOG2E - row_lse)
    return dual_prices * gain[:, :SLOTS], fill_rate


def solution(mesh):
    split = Mesh(mesh.devices.reshape(NX, NZ, NY, NC), ("x", "z", "y", "core"))
    wide, narrow = ("x", "z"), ("y", "core")
    placed = (
        P(wide, None),
        P(narrow, None),
        P(narrow),
        P(narrow + wide, None),
        P(narrow + wide, None),
        P(wide),
        P(wide),
    )
    return jax.shard_map(
        shards,
        mesh=split,
        in_specs=placed,
        out_specs=(P(narrow + wide, None), P(wide)),
        check_vma=False,
    )
```

```python
import math

import jax
import jax.numpy as jnp
from jax import lax
from jax.experimental import pallas as pl
from jax.experimental.pallas import tpu as pltpu
from jax.sharding import Mesh, PartitionSpec as P

SLOTS = 96
ITERS = 2
LOG2E = math.log2(math.e)
SCALE = 0.375
TO_LOG2 = SCALE * LOG2E
NX, NZ, NY, NC = 4, 8, 4, 2
LANES = 128
HALF = 512
PACK_ROWS = 80
OWNED = 200
NEAR = NX * OWNED
CAMPS = NC * NEAR
IMPS = NZ * HALF
ROWS = IMPS // LANES
COLS = 256
PIECE = 80
SENT = 4.0
VMEM_LIMIT = 8 * 1024 * 1024
f32, bf16 = jnp.float32, jnp.bfloat16
VMEM = pltpu.VMEM


def shifted(value, axis, size, step):
    return lax.ppermute(value, axis, [(i, (i + step) % size) for i in range(size)])


def in_vmem(kernel, outs, scratch, *operands):
    whole = pl.BlockSpec(memory_space=VMEM)
    return pl.pallas_call(
        kernel,
        in_specs=[whole] * len(operands),
        out_specs=[whole] * len(outs),
        out_shape=[VMEM(shape, dtype) for shape, dtype in outs],
        scratch_shapes=[VMEM(shape, dtype) for shape, dtype in scratch],
        compiler_params=pltpu.CompilerParams(vmem_limit_bytes=VMEM_LIMIT),
    )(*operands)


def one_hot_rows(slot_tile):
    slot_row = slot_tile.astype(f32)[0:1, :]
    return lax.broadcasted_iota(jnp.int32, (SLOTS, slot_row.shape[1]), 0).astype(f32) == slot_row


def folded(value, op):
    parts = [value[r : r + 8] for r in range(0, value.shape[0], 8)]
    total = parts[0]
    for part in parts[1:]:
        total = op(total, part)
    return total


def joined(ref, first, count):
    return jnp.concatenate([ref[pl.ds(first + r, 1), :] for r in range(count)], axis=1)


def stats_kernel(pack_ref, priced_ref, camps_ref, reserve_ref, even_ref, odd_ref, lse_ref, hot_ref, left, right0, right1):
    rights, halves = (right0, right1), (even_ref, odd_ref)
    per_block = COLS // LANES
    for r in range(0, CAMPS, 160):
        rows = slice(r, r + 160)
        high = priced_ref[rows].astype(bf16)
        low = (priced_ref[rows] - high.astype(f32)).astype(bf16)
        left[rows, :LANES] = high + camps_ref[rows, :LANES]
        left[rows, LANES:] = low + camps_ref[rows, LANES:]
    hot_ref[SLOTS:, :] = jnp.zeros((LANES - SLOTS, IMPS), bf16)

    def logits(z, h):
        right, cols = rights[h], slice(h * COLS, (h + 1) * COLS)
        hot = one_hot_rows(pack_ref[z, 64:80, cols]).astype(f32).astype(bf16)
        hot_ref[0:SLOTS, pl.ds(pl.multiple_of(z * HALF + h * COLS, COLS), COLS)] = hot
        right[0:96, :] = hot
        right[96:128, :] = pack_ref[z, 0:32, cols]
        right[128:224, :] = hot
        right[224:256, :] = pack_ref[z, 32:64, cols]
        halves[h][z] = jnp.dot(left[...], right[...], preferred_element_type=f32)

    def top(z, h):
        best = folded(halves[h][z, 0:PIECE], jnp.maximum)
        for r in range(PIECE, CAMPS, PIECE):
            best = jnp.maximum(best, folded(halves[h][z, r : r + PIECE], jnp.maximum))
        return jnp.max(best, axis=0, keepdims=True)

    def weigh(z, h, best):
        first = (z * 2 + h) * per_block
        reserve = joined(reserve_ref, first, per_block)
        peak = jnp.maximum(best * TO_LOG2, reserve)
        total = jnp.zeros((8, COLS), f32)
        for r in range(0, CAMPS, PIECE):
            weights = jnp.exp2(halves[h][z, r : r + PIECE] * TO_LOG2 - peak)
            total = total + folded(weights, jnp.add)
        total = jnp.sum(total, axis=0, keepdims=True) + jnp.exp2(reserve - peak)
        lse = peak + jnp.log2(total)
        for r in range(per_block):
            lse_ref[pl.ds(first + r, 1), :] = lse[:, r * LANES : (r + 1) * LANES]

    def both(z, best0):
        logits(z, 1)
        weigh(z, 0, best0)
        best1 = top(z, 1)
        if z + 1 < NZ:
            logits(z + 1, 0)
        weigh(z, 1, best1)
        return top(z + 1, 0) if z + 1 < NZ else None

    logits(0, 0)
    best = top(0, 0)
    for z in range(NZ):
        best = both(z, best)


def local_stats(pack, priced, camps, reserve):
    return in_vmem(
        stats_kernel,
        [((NZ, CAMPS, COLS), f32)] * 2 + [((ROWS, LANES), f32), ((LANES, IMPS), bf16)],
        [((CAMPS, 2 * LANES), bf16), ((2 * LANES, COLS), bf16), ((2 * LANES, COLS), bf16)],
        pack, priced, camps, reserve,
    )


def merged(pieces):
    top = pieces[0]
    for piece in pieces[1:]:
        top = jnp.maximum(top, piece)
    return top + jnp.log2(sum(jnp.exp2(piece - top) for piece in pieces))


def spent(first, even_ref, odd_ref, hot_ref, lse_ref, spend_ref, weights0, weights1):
    def columns(z):
        return pl.ds(pl.multiple_of(z * HALF, HALF), HALF)

    def weigh(z, weights):
        per_block = COLS // LANES
        for h, logits_ref in enumerate((even_ref, odd_ref)):
            lse = joined(lse_ref, (z * 2 + h) * per_block, per_block)
            for r in range(0, NEAR, PIECE):
                logits = logits_ref[z, first + r : first + r + PIECE]
                weights[r : r + PIECE, h * COLS : (h + 1) * COLS] = jnp.exp2(
                    logits * TO_LOG2 - lse
                ).astype(bf16)

    def gather(z, weights):
        spend_ref[...] += lax.dot_general(
            weights[...], hot_ref[:, columns(z)], (((1,), (1,)), ((), ())), preferred_element_type=f32
        )

    def both(k, carry):
        gather(2 * k, weights0)
        weigh(2 * k + 1, weights1)
        gather(2 * k + 1, weights1)
        weigh(jnp.minimum(2 * k + 2, NZ - 1), weights0)
        return carry

    spend_ref[...] = jnp.zeros(spend_ref.shape, f32)
    weigh(0, weights0)
    lax.fori_loop(0, NZ // 2, both, 0)


def far_kernel(even_ref, odd_ref, hot_ref, parts_ref, far_ref, lse_ref, weights0, weights1):
    lse_ref[...] = merged([parts_ref[k] for k in range(NZ)])
    spent(NEAR, even_ref, odd_ref, hot_ref, lse_ref, far_ref, weights0, weights1)


def near_kernel(*refs):
    spent(0, *refs)


def joint_kernel(even_ref, odd_ref, hot_ref, parts_ref, far_ref, near_ref, lse_ref, *weights):
    lse_ref[...] = merged([parts_ref[k] for k in range(NZ)])
    spent(NEAR, even_ref, odd_ref, hot_ref, lse_ref, far_ref, *weights)
    spent(0, even_ref, odd_ref, hot_ref, lse_ref, near_ref, *weights)


WEIGHTS = [((NEAR, HALF), bf16)] * 2


def far_spend(even, odd, hot, parts):
    return in_vmem(
        far_kernel, [((NEAR, LANES), f32), ((ROWS, LANES), f32)], WEIGHTS, even, odd, hot, parts
    )


def joint_spend(even, odd, hot, parts):
    return in_vmem(
        joint_kernel,
        [((NEAR, LANES), f32)] * 2 + [((ROWS, LANES), f32)],
        WEIGHTS,
        even, odd, hot, parts,
    )


def near_spend(even, odd, hot, lse):
    return in_vmem(near_kernel, [((NEAR, LANES), f32)], WEIGHTS, even, odd, hot, lse)[0]


def landed(sources, targets, sems):
    copies = [
        pltpu.make_async_copy(source, target, sems.at[k])
        for k, (source, target) in enumerate(zip(sources, targets))
    ]
    for copy in copies:
        copy.start()
    for copy in copies:
        copy.wait()


def pack_kernel(users_hbm, slots_hbm, packs_ref, token_ref, users_ref, slots_ref, sems):
    landed((users_hbm, slots_hbm), (users_ref, slots_ref), sems)
    near = lax.axis_index("core") == 0
    users = jnp.where(near, users_ref[:, :HALF].astype(f32), users_ref[:, HALF:].astype(f32))
    half = HALF // LANES
    slots = jnp.where(near, slots_ref[:half], slots_ref[half:]).astype(f32)
    slots = jnp.concatenate([slots[r : r + 1] for r in range(half)], axis=1)
    tail = jnp.broadcast_to(slots, (PACK_ROWS - 64, HALF)).astype(bf16)
    for k in range(NZ):
        packs_ref[k, 0:64, :] = users.astype(bf16)
        packs_ref[k, 64:80, :] = tail
    token_ref[...] = slots_ref[...].astype(f32)


def state_kernel(duals_hbm, targets_hbm, after, state_ref, duals_ref, targets_ref, square, sems):
    landed((duals_hbm, targets_hbm), (duals_ref, targets_ref), sems)
    square[...] = jnp.zeros(square.shape, f32)
    square[0:SLOTS, 0:OWNED] = duals_ref[...]
    state_ref[:, :LANES] = square[...].T[:OWNED]
    square[0:SLOTS, 0:OWNED] = 0.5 / targets_ref[...]
    state_ref[:, LANES:] = square[...].T[:OWNED]


def from_hbm(kernel, outs, scratch, operands, *after):
    operands = [pltpu.with_memory_space_constraint(a, pltpu.HBM) for a in operands]
    hbm, vmem = pl.BlockSpec(memory_space=pltpu.HBM), pl.BlockSpec(memory_space=VMEM)
    return pl.pallas_call(
        kernel,
        in_specs=[hbm] * len(operands) + [vmem] * len(after),
        out_specs=[vmem] * len(outs),
        out_shape=[VMEM(*out) for out in outs],
        scratch_shapes=[VMEM(a.shape, a.dtype) for a in operands]
        + scratch
        + [pltpu.SemaphoreType.DMA((len(operands),))],
        compiler_params=pltpu.CompilerParams(vmem_limit_bytes=VMEM_LIMIT),
    )(*operands, *after)


def near_rows(array, x, z):
    starts = [((x + NX - s) % NX) * (NZ * OWNED) + z * OWNED for s in range(NX)]
    return jnp.concatenate([lax.dynamic_slice_in_dim(array, at, OWNED, 0) for at in starts])


def both_cores(near):
    return jnp.concatenate([near, shifted(near, "core", NC, 1)])


def over_x(owned):
    return jnp.concatenate([owned] + [shifted(owned, "x", NX, s) for s in range(1, NX)])


def shards(user_vectors, campaigns, campaign_bids, spend_targets, dual_prices, slot_index, reserve):
    x, z, y, core = (lax.axis_index(a) for a in ("x", "z", "y", "core"))
    pack, token = from_hbm(
        pack_kernel,
        [((NZ, PACK_ROWS, HALF), bf16), ((8, LANES), f32)],
        [],
        (user_vectors.T, slot_index.reshape(-1, LANES)),
    )
    pack = lax.all_to_all(pack, "z", 0, 0, tiled=True)
    token = shifted(token, "core", NC, 1)
    (state,) = from_hbm(
        state_kernel,
        [((OWNED, 2 * LANES), f32)],
        [VMEM((LANES, 2 * LANES), f32)],
        (dual_prices.T, spend_targets.T),
        token,
    )
    z_late, state = lax.optimization_barrier((z, state))
    state = over_x(state)
    camps = both_cores(near_rows(campaigns, x, z_late))
    blank = jnp.zeros((CAMPS, SLOTS), bf16)
    camps = jnp.concatenate([blank, camps[:, :32], blank, camps[:, 32:]], axis=1)
    bids = near_rows(campaign_bids, x, z_late)[:, None]
    priced, rates = state[:, :LANES] * (bids * (-1.0 / SCALE)), state[:, LANES:] * bids

    own_reserve = (
        lax.dynamic_slice_in_dim(reserve, core * HALF, HALF, 0) * LOG2E
    ).reshape(1, HALF // LANES, LANES)
    at_home = (lax.broadcasted_iota(jnp.int32, (NZ, 1, 1), 0) == z) & (y == 0)
    wide_reserve = jnp.where(at_home, own_reserve, -1e30).reshape(ROWS, LANES)

    gain = 1.0
    for step in range(ITERS):
        even, odd, lse, hot = local_stats(pack, both_cores(priced), camps, wide_reserve)
        lse = merged([lse] + [shifted(lse, "y", NY, s) for s in range(1, NY)])
        parts = lax.all_to_all(
            jnp.broadcast_to(lse[None], (NZ, ROWS, LANES)), "z", 0, 0, tiled=True
        )
        if step + 1 < ITERS:
            far, lse = far_spend(even, odd, hot, parts)
            far = shifted(far, "core", NC, 1)
            near = near_spend(even, odd, hot, lse)
        else:
            far, near, lse = joint_spend(even, odd, hot, parts)
            far = shifted(far, "core", NC, 1)
        spend = near + far
        sent = (spend * SENT).astype(jnp.float16)
        if step + 1 < ITERS:
            for s in range(1, NX):
                spend = spend + jnp.roll(shifted(sent, "x", NX, s), s * OWNED, 0).astype(f32) * (1.0 / SENT)
            factor = jnp.sqrt(0.5 + spend * rates)
            priced = priced * factor
            gain = factor[:OWNED]
        else:
            own = spend[:OWNED]
            for s in range(1, NX):
                block = shifted(sent[s * OWNED : (s + 1) * OWNED], "x", NX, -s)
                own = own + block.astype(f32) * (1.0 / SENT)
            gain = gain * jnp.sqrt(0.5 + own * rates[:OWNED])

    home = lax.dynamic_slice_in_dim(lse.reshape(NZ, HALF), z, 1, 0).reshape(HALF)
    far = shifted(home, "core", NC, 1)
    row_lse = jnp.where(core == 0, jnp.concatenate([home, far]), jnp.concatenate([far, home]))
    fill_rate = 1.0 - jnp.exp2(reserve * LOG2E - row_lse)
    return dual_prices * gain[:, :SLOTS], fill_rate


def solution(mesh):
    split = Mesh(mesh.devices.reshape(NX, NZ, NY, NC), ("x", "z", "y", "core"))
    wide, narrow = ("x", "z"), ("y", "core")
    placed = (
        P(wide, None),
        P(narrow, None),
        P(narrow),
        P(narrow + wide, None),
        P(narrow + wide, None),
        P(wide),
        P(wide),
    )
    return jax.shard_map(
        shards,
        mesh=split,
        in_specs=placed,
        out_specs=(P(narrow + wide, None), P(wide)),
        check_vma=False,
    )
```

```python
import math

import jax
import jax.numpy as jnp
from jax import lax
from jax.experimental import pallas as pl
from jax.experimental.pallas import tpu as pltpu
from jax.sharding import Mesh, PartitionSpec as P

SLOTS = 96
ITERS = 2
LOG2E = math.log2(math.e)
SCALE = 0.375
TO_LOG2 = SCALE * LOG2E
NX, NZ, NY, NC = 4, 8, 4, 2
LANES = 128
HALF = 512
PACK_ROWS = 80
OWNED = 200
NEAR = NX * OWNED
THIN = 152
REST = OWNED - THIN
CAMPS = NC * NEAR
IMPS = NZ * HALF
ROWS = IMPS // LANES
COLS = 256
PIECE = 80
SENT = 4.0
VMEM_LIMIT = 8 * 1024 * 1024
f32, bf16 = jnp.float32, jnp.bfloat16
VMEM = pltpu.VMEM


def shifted(value, axis, size, step):
    return lax.ppermute(value, axis, [(i, (i + step) % size) for i in range(size)])


def in_vmem(kernel, outs, scratch, *operands):
    whole = pl.BlockSpec(memory_space=VMEM)
    return pl.pallas_call(
        kernel,
        in_specs=[whole] * len(operands),
        out_specs=[whole] * len(outs),
        out_shape=[VMEM(shape, dtype) for shape, dtype in outs],
        scratch_shapes=[VMEM(shape, dtype) for shape, dtype in scratch],
        compiler_params=pltpu.CompilerParams(vmem_limit_bytes=VMEM_LIMIT),
    )(*operands)


def one_hot_rows(slot_tile):
    slot_row = slot_tile.astype(f32)[0:1, :]
    return lax.broadcasted_iota(jnp.int32, (SLOTS, slot_row.shape[1]), 0).astype(f32) == slot_row


def folded(value, op):
    parts = [value[r : r + 8] for r in range(0, value.shape[0], 8)]
    total = parts[0]
    for part in parts[1:]:
        total = op(total, part)
    return total


def joined(ref, first, count):
    return jnp.concatenate([ref[pl.ds(first + r, 1), :] for r in range(count)], axis=1)


def stats_kernel(pack_ref, priced_ref, camps_ref, reserve_ref, even_ref, odd_ref, lse_ref, hot_ref, left, right0, right1):
    rights, halves = (right0, right1), (even_ref, odd_ref)
    per_block = COLS // LANES
    for r in range(0, CAMPS, 160):
        rows = slice(r, r + 160)
        high = priced_ref[rows].astype(bf16)
        low = (priced_ref[rows] - high.astype(f32)).astype(bf16)
        left[rows, :LANES] = high + camps_ref[rows, :LANES]
        left[rows, LANES:] = low + camps_ref[rows, LANES:]
    hot_ref[SLOTS:, :] = jnp.zeros((LANES - SLOTS, IMPS), bf16)

    def logits(z, h):
        right, cols = rights[h], slice(h * COLS, (h + 1) * COLS)
        hot = one_hot_rows(pack_ref[z, 64:80, cols]).astype(f32).astype(bf16)
        hot_ref[0:SLOTS, pl.ds(pl.multiple_of(z * HALF + h * COLS, COLS), COLS)] = hot
        right[0:96, :] = hot
        right[96:128, :] = pack_ref[z, 0:32, cols]
        right[128:224, :] = hot
        right[224:256, :] = pack_ref[z, 32:64, cols]
        halves[h][z] = jnp.dot(left[...], right[...], preferred_element_type=f32)

    def top(z, h):
        best = folded(halves[h][z, 0:PIECE], jnp.maximum)
        for r in range(PIECE, CAMPS, PIECE):
            best = jnp.maximum(best, folded(halves[h][z, r : r + PIECE], jnp.maximum))
        return jnp.max(best, axis=0, keepdims=True)

    def weigh(z, h, best):
        first = (z * 2 + h) * per_block
        reserve = joined(reserve_ref, first, per_block)
        peak = jnp.maximum(best * TO_LOG2, reserve)
        total = jnp.zeros((8, COLS), f32)
        for r in range(0, CAMPS, PIECE):
            weights = jnp.exp2(halves[h][z, r : r + PIECE] * TO_LOG2 - peak)
            total = total + folded(weights, jnp.add)
        total = jnp.sum(total, axis=0, keepdims=True) + jnp.exp2(reserve - peak)
        lse = peak + jnp.log2(total)
        for r in range(per_block):
            lse_ref[pl.ds(first + r, 1), :] = lse[:, r * LANES : (r + 1) * LANES]

    def both(z, best0):
        logits(z, 1)
        weigh(z, 0, best0)
        best1 = top(z, 1)
        if z + 1 < NZ:
            logits(z + 1, 0)
        weigh(z, 1, best1)
        return top(z + 1, 0) if z + 1 < NZ else None

    logits(0, 0)
    best = top(0, 0)
    for z in range(NZ):
        best = both(z, best)


def local_stats(pack, priced, camps, reserve):
    return in_vmem(
        stats_kernel,
        [((NZ, CAMPS, COLS), f32)] * 2 + [((ROWS, LANES), f32), ((LANES, IMPS), bf16)],
        [((CAMPS, 2 * LANES), bf16), ((2 * LANES, COLS), bf16), ((2 * LANES, COLS), bf16)],
        pack, priced, camps, reserve,
    )


def merged(pieces):
    top = pieces[0]
    for piece in pieces[1:]:
        top = jnp.maximum(top, piece)
    return top + jnp.log2(sum(jnp.exp2(piece - top) for piece in pieces))


def spent(first, even_ref, odd_ref, hot_ref, lse_ref, spend_ref, weights0, weights1):
    def columns(z):
        return pl.ds(pl.multiple_of(z * HALF, HALF), HALF)

    def weigh(z, weights):
        per_block = COLS // LANES
        for h, logits_ref in enumerate((even_ref, odd_ref)):
            lse = joined(lse_ref, (z * 2 + h) * per_block, per_block)
            for r in range(0, NEAR, PIECE):
                logits = logits_ref[z, first + r : first + r + PIECE]
                weights[r : r + PIECE, h * COLS : (h + 1) * COLS] = jnp.exp2(
                    logits * TO_LOG2 - lse
                ).astype(bf16)

    def gather(z, weights):
        spend_ref[...] += lax.dot_general(
            weights[...], hot_ref[:, columns(z)], (((1,), (1,)), ((), ())), preferred_element_type=f32
        )

    def both(k, carry):
        gather(2 * k, weights0)
        weigh(2 * k + 1, weights1)
        gather(2 * k + 1, weights1)
        weigh(jnp.minimum(2 * k + 2, NZ - 1), weights0)
        return carry

    spend_ref[...] = jnp.zeros(spend_ref.shape, f32)
    weigh(0, weights0)
    lax.fori_loop(0, NZ // 2, both, 0)


def far_kernel(even_ref, odd_ref, hot_ref, parts_ref, far_ref, lse_ref, weights0, weights1):
    lse_ref[...] = merged([parts_ref[k] for k in range(NZ)])
    spent(NEAR, even_ref, odd_ref, hot_ref, lse_ref, far_ref, weights0, weights1)


def near_kernel(*refs):
    spent(0, *refs)


def joint_kernel(even_ref, odd_ref, hot_ref, parts_ref, far_ref, near_ref, lse_ref, *weights):
    lse_ref[...] = merged([parts_ref[k] for k in range(NZ)])
    spent(NEAR, even_ref, odd_ref, hot_ref, lse_ref, far_ref, *weights)
    spent(0, even_ref, odd_ref, hot_ref, lse_ref, near_ref, *weights)


WEIGHTS = [((NEAR, HALF), bf16)] * 2


def far_spend(even, odd, hot, parts):
    return in_vmem(
        far_kernel, [((NEAR, LANES), f32), ((ROWS, LANES), f32)], WEIGHTS, even, odd, hot, parts
    )


def joint_spend(even, odd, hot, parts):
    return in_vmem(
        joint_kernel,
        [((NEAR, LANES), f32)] * 2 + [((ROWS, LANES), f32)],
        WEIGHTS,
        even, odd, hot, parts,
    )


def near_spend(even, odd, hot, lse):
    return in_vmem(near_kernel, [((NEAR, LANES), f32)], WEIGHTS, even, odd, hot, lse)[0]


def lanes_of(rows):
    return lax.broadcasted_iota(jnp.int32, (rows, LANES), 1)


def thinned(wide, thin_ref, at, col):
    spare = lanes_of(REST) >= SLOTS
    rest = wide[THIN:OWNED]
    for j in range(3):
        moved = jnp.where(spare, pltpu.roll(rest, SLOTS - 32 * j, 1), 0.0)
        thin_ref[at + j * REST : at + (j + 1) * REST, col] = wide[j * REST : (j + 1) * REST] + moved
    thin_ref[at + 3 * REST : at + THIN, col] = wide[3 * REST : THIN]


def thin_kernel(first, second, thin_ref):
    for k in range(first.shape[0] // OWNED):
        rows = slice(k * OWNED, (k + 1) * OWNED)
        thinned(first[rows] + second[rows], thin_ref, k * THIN, slice(0, LANES))


def wide_kernel(thin_ref, wide_ref):
    lanes = lanes_of(REST)
    for k in range(thin_ref.shape[0] // THIN):
        thin = thin_ref[k * THIN : (k + 1) * THIN]
        wide_ref[k * OWNED : k * OWNED + THIN] = jnp.where(lanes_of(THIN) < SLOTS, thin, 0.0)
        rest = jnp.zeros((REST, LANES), f32)
        for j in range(3):
            moved = pltpu.roll(thin[j * REST : (j + 1) * REST], 32 + 32 * j, 1)
            rest = jnp.where((lanes >= 32 * j) & (lanes < 32 * j + 32), moved, rest)
        wide_ref[k * OWNED + THIN : (k + 1) * OWNED] = rest


def as_thin(first, second):
    rows = first.shape[0] // OWNED * THIN
    return in_vmem(thin_kernel, [((rows, LANES), f32)], [], first, second)[0]


def as_wide(thin):
    rows = thin.shape[0] // THIN * OWNED
    return in_vmem(wide_kernel, [((rows, LANES), f32)], [], thin)[0]


def landed(sources, targets, sems):
    copies = [
        pltpu.make_async_copy(source, target, sems.at[k])
        for k, (source, target) in enumerate(zip(sources, targets))
    ]
    for copy in copies:
        copy.start()
    for copy in copies:
        copy.wait()


def pack_kernel(users_hbm, slots_hbm, packs_ref, token_ref, users_ref, slots_ref, sems):
    landed((users_hbm, slots_hbm), (users_ref, slots_ref), sems)
    near = lax.axis_index("core") == 0
    users = jnp.where(near, users_ref[:, :HALF].astype(f32), users_ref[:, HALF:].astype(f32))
    half = HALF // LANES
    slots = jnp.where(near, slots_ref[:half], slots_ref[half:]).astype(f32)
    slots = jnp.concatenate([slots[r : r + 1] for r in range(half)], axis=1)
    tail = jnp.broadcast_to(slots, (PACK_ROWS - 64, HALF)).astype(bf16)
    for k in range(NZ):
        packs_ref[k, 0:64, :] = users.astype(bf16)
        packs_ref[k, 64:80, :] = tail
    token_ref[...] = slots_ref[...].astype(f32)


def state_kernel(duals_hbm, targets_hbm, after, state_ref, duals_ref, targets_ref, square, sems):
    landed((duals_hbm, targets_hbm), (duals_ref, targets_ref), sems)
    square[...] = jnp.zeros(square.shape, f32)
    square[0:SLOTS, 0:OWNED] = duals_ref[...]
    thinned(square[...].T[:OWNED], state_ref, 0, slice(0, LANES))
    square[0:SLOTS, 0:OWNED] = 0.5 / targets_ref[...]
    thinned(square[...].T[:OWNED], state_ref, 0, slice(LANES, 2 * LANES))


def from_hbm(kernel, outs, scratch, operands, *after):
    operands = [pltpu.with_memory_space_constraint(a, pltpu.HBM) for a in operands]
    hbm, vmem = pl.BlockSpec(memory_space=pltpu.HBM), pl.BlockSpec(memory_space=VMEM)
    return pl.pallas_call(
        kernel,
        in_specs=[hbm] * len(operands) + [vmem] * len(after),
        out_specs=[vmem] * len(outs),
        out_shape=[VMEM(*out) for out in outs],
        scratch_shapes=[VMEM(a.shape, a.dtype) for a in operands]
        + scratch
        + [pltpu.SemaphoreType.DMA((len(operands),))],
        compiler_params=pltpu.CompilerParams(vmem_limit_bytes=VMEM_LIMIT),
    )(*operands, *after)


def near_rows(array, x, z):
    starts = [((x + NX - s) % NX) * (NZ * OWNED) + z * OWNED for s in range(NX)]
    return jnp.concatenate([lax.dynamic_slice_in_dim(array, at, OWNED, 0) for at in starts])


def both_cores(near):
    return jnp.concatenate([near, shifted(near, "core", NC, 1)])


def over_x(owned):
    return jnp.concatenate([owned] + [shifted(owned, "x", NX, s) for s in range(1, NX)])


def shards(user_vectors, campaigns, campaign_bids, spend_targets, dual_prices, slot_index, reserve):
    x, z, y, core = (lax.axis_index(a) for a in ("x", "z", "y", "core"))
    pack, token = from_hbm(
        pack_kernel,
        [((NZ, PACK_ROWS, HALF), bf16), ((8, LANES), f32)],
        [],
        (user_vectors.T, slot_index.reshape(-1, LANES)),
    )
    pack = lax.all_to_all(pack, "z", 0, 0, tiled=True)
    token = shifted(token, "core", NC, 1)
    (state,) = from_hbm(
        state_kernel,
        [((THIN, 2 * LANES), f32)],
        [VMEM((LANES, 2 * LANES), f32)],
        (dual_prices.T, spend_targets.T),
        token,
    )
    z_late, state = lax.optimization_barrier((z, state))
    state = over_x(state)
    camps = both_cores(near_rows(campaigns, x, z_late))
    blank = jnp.zeros((CAMPS, SLOTS), bf16)
    camps = jnp.concatenate([blank, camps[:, :32], blank, camps[:, 32:]], axis=1)
    bids = jnp.broadcast_to(near_rows(campaign_bids, x, z_late)[:, None], (NEAR, LANES))
    bids = jnp.where(lax.broadcasted_iota(jnp.int32, (NEAR, LANES), 1) < SLOTS, bids, 0.0)
    bids = as_thin(bids, jnp.zeros((NEAR, LANES), f32))
    priced, rates = state[:, :LANES] * (bids * (-1.0 / SCALE)), state[:, LANES:] * bids

    own_reserve = (
        lax.dynamic_slice_in_dim(reserve, core * HALF, HALF, 0) * LOG2E
    ).reshape(1, HALF // LANES, LANES)
    at_home = (lax.broadcasted_iota(jnp.int32, (NZ, 1, 1), 0) == z) & (y == 0)
    wide_reserve = jnp.where(at_home, own_reserve, -1e30).reshape(ROWS, LANES)

    gain = 1.0
    for step in range(ITERS):
        even, odd, lse, hot = local_stats(pack, as_wide(both_cores(priced)), camps, wide_reserve)
        lse = merged([lse] + [shifted(lse, "y", NY, s) for s in range(1, NY)])
        parts = lax.all_to_all(
            jnp.broadcast_to(lse[None], (NZ, ROWS, LANES)), "z", 0, 0, tiled=True
        )
        if step + 1 < ITERS:
            far, lse = far_spend(even, odd, hot, parts)
            far = shifted(far, "core", NC, 1)
            near = near_spend(even, odd, hot, lse)
        else:
            far, near, lse = joint_spend(even, odd, hot, parts)
            far = shifted(far, "core", NC, 1)
        spend = as_thin(near, far)
        sent = (spend * SENT).astype(jnp.float16)
        if step + 1 < ITERS:
            for s in range(1, NX):
                spend = spend + jnp.roll(shifted(sent, "x", NX, s), s * THIN, 0).astype(f32) * (1.0 / SENT)
            factor = jnp.sqrt(0.5 + spend * rates)
            priced = priced * factor
            gain = factor[:THIN]
        else:
            own = spend[:THIN]
            for s in range(1, NX):
                block = shifted(sent[s * THIN : (s + 1) * THIN], "x", NX, -s)
                own = own + block.astype(f32) * (1.0 / SENT)
            gain = gain * jnp.sqrt(0.5 + own * rates[:THIN])

    home = lax.dynamic_slice_in_dim(lse.reshape(NZ, HALF), z, 1, 0).reshape(HALF)
    far = shifted(home, "core", NC, 1)
    row_lse = jnp.where(core == 0, jnp.concatenate([home, far]), jnp.concatenate([far, home]))
    fill_rate = 1.0 - jnp.exp2(reserve * LOG2E - row_lse)
    return dual_prices * as_wide(gain)[:, :SLOTS], fill_rate


def solution(mesh):
    split = Mesh(mesh.devices.reshape(NX, NZ, NY, NC), ("x", "z", "y", "core"))
    wide, narrow = ("x", "z"), ("y", "core")
    placed = (
        P(wide, None),
        P(narrow, None),
        P(narrow),
        P(narrow + wide, None),
        P(narrow + wide, None),
        P(wide),
        P(wide),
    )
    return jax.shard_map(
        shards,
        mesh=split,
        in_specs=placed,
        out_specs=(P(narrow + wide, None), P(wide)),
        check_vma=False,
    )
```

```python
import math

import jax
import jax.numpy as jnp
from jax import lax
from jax.experimental import pallas as pl
from jax.experimental.pallas import tpu as pltpu
from jax.sharding import Mesh, PartitionSpec as P

SLOTS = 96
ITERS = 2
LOG2E = math.log2(math.e)
SCALE = 0.375
TO_LOG2 = SCALE * LOG2E
NX, NZ, NY, NC = 4, 8, 4, 2
LANES = 128
HALF = 512
PACK_ROWS = 80
OWNED = 200
NEAR = NX * OWNED
THIN = 152
REST = OWNED - THIN
CAMPS = NC * NEAR
IMPS = NZ * HALF
ROWS = IMPS // LANES
COLS = 256
PIECE = 80
SENT = 4.0
VMEM_LIMIT = 8 * 1024 * 1024
f32, bf16 = jnp.float32, jnp.bfloat16
VMEM = pltpu.VMEM


def shifted(value, axis, size, step):
    return lax.ppermute(value, axis, [(i, (i + step) % size) for i in range(size)])


def in_vmem(kernel, outs, scratch, *operands):
    whole = pl.BlockSpec(memory_space=VMEM)
    return pl.pallas_call(
        kernel,
        in_specs=[whole] * len(operands),
        out_specs=[whole] * len(outs),
        out_shape=[VMEM(shape, dtype) for shape, dtype in outs],
        scratch_shapes=[VMEM(shape, dtype) for shape, dtype in scratch],
        compiler_params=pltpu.CompilerParams(vmem_limit_bytes=VMEM_LIMIT),
    )(*operands)


def one_hot_rows(slot_tile):
    slot_row = slot_tile.astype(f32)[0:1, :]
    return lax.broadcasted_iota(jnp.int32, (SLOTS, slot_row.shape[1]), 0).astype(f32) == slot_row


def folded(value, op):
    parts = [value[r : r + 8] for r in range(0, value.shape[0], 8)]
    total = parts[0]
    for part in parts[1:]:
        total = op(total, part)
    return total


def joined(ref, first, count):
    return jnp.concatenate([ref[pl.ds(first + r, 1), :] for r in range(count)], axis=1)


def stats_kernel(pack_ref, priced_ref, camps_ref, reserve_ref, even_ref, odd_ref, lse_ref, hot_ref, left, right0, right1):
    rights, halves = (right0, right1), (even_ref, odd_ref)
    per_block = COLS // LANES
    for r in range(0, CAMPS, 160):
        rows = slice(r, r + 160)
        high = priced_ref[rows].astype(bf16)
        low = (priced_ref[rows] - high.astype(f32)).astype(bf16)
        left[rows, :LANES] = high + camps_ref[rows, :LANES]
        left[rows, LANES:] = low + camps_ref[rows, LANES:]
    hot_ref[SLOTS:, :] = jnp.zeros((LANES - SLOTS, IMPS), bf16)

    def logits(z, h):
        right, cols = rights[h], slice(h * COLS, (h + 1) * COLS)
        hot = one_hot_rows(pack_ref[z, 64:80, cols]).astype(f32).astype(bf16)
        hot_ref[0:SLOTS, pl.ds(pl.multiple_of(z * HALF + h * COLS, COLS), COLS)] = hot
        right[0:96, :] = hot
        right[96:128, :] = pack_ref[z, 0:32, cols]
        right[128:224, :] = hot
        right[224:256, :] = pack_ref[z, 32:64, cols]
        halves[h][z] = jnp.dot(left[...], right[...], preferred_element_type=f32)

    def top(z, h):
        best = folded(halves[h][z, 0:PIECE], jnp.maximum)
        for r in range(PIECE, CAMPS, PIECE):
            best = jnp.maximum(best, folded(halves[h][z, r : r + PIECE], jnp.maximum))
        return jnp.max(best, axis=0, keepdims=True)

    def weigh(z, h, best):
        first = (z * 2 + h) * per_block
        reserve = joined(reserve_ref, first, per_block)
        peak = jnp.maximum(best * TO_LOG2, reserve)
        total = jnp.zeros((8, COLS), f32)
        for r in range(0, CAMPS, PIECE):
            weights = jnp.exp2(halves[h][z, r : r + PIECE] * TO_LOG2 - peak)
            total = total + folded(weights, jnp.add)
        total = jnp.sum(total, axis=0, keepdims=True) + jnp.exp2(reserve - peak)
        lse = peak + jnp.log2(total)
        for r in range(per_block):
            lse_ref[pl.ds(first + r, 1), :] = lse[:, r * LANES : (r + 1) * LANES]

    def both(z, best0):
        logits(z, 1)
        weigh(z, 0, best0)
        best1 = top(z, 1)
        if z + 1 < NZ:
            logits(z + 1, 0)
        weigh(z, 1, best1)
        return top(z + 1, 0) if z + 1 < NZ else None

    logits(0, 0)
    best = top(0, 0)
    for z in range(NZ):
        best = both(z, best)


def local_stats(pack, priced, camps, reserve):
    return in_vmem(
        stats_kernel,
        [((NZ, CAMPS, COLS), f32)] * 2 + [((ROWS, LANES), f32), ((LANES, IMPS), bf16)],
        [((CAMPS, 2 * LANES), bf16), ((2 * LANES, COLS), bf16), ((2 * LANES, COLS), bf16)],
        pack, priced, camps, reserve,
    )


def merged(pieces):
    top = pieces[0]
    for piece in pieces[1:]:
        top = jnp.maximum(top, piece)
    return top + jnp.log2(sum(jnp.exp2(piece - top) for piece in pieces))


def spent(first, even_ref, odd_ref, hot_ref, lse_ref, spend_ref, weights0, weights1):
    def columns(z):
        return pl.ds(pl.multiple_of(z * HALF, HALF), HALF)

    def weigh(z, weights):
        per_block = COLS // LANES
        for h, logits_ref in enumerate((even_ref, odd_ref)):
            lse = joined(lse_ref, (z * 2 + h) * per_block, per_block)
            for r in range(0, NEAR, PIECE):
                logits = logits_ref[z, first + r : first + r + PIECE]
                weights[r : r + PIECE, h * COLS : (h + 1) * COLS] = jnp.exp2(
                    logits * TO_LOG2 - lse
                ).astype(bf16)

    def gather(z, weights):
        spend_ref[...] += lax.dot_general(
            weights[...], hot_ref[:, columns(z)], (((1,), (1,)), ((), ())), preferred_element_type=f32
        )

    def both(k, carry):
        gather(2 * k, weights0)
        weigh(2 * k + 1, weights1)
        gather(2 * k + 1, weights1)
        weigh(jnp.minimum(2 * k + 2, NZ - 1), weights0)
        return carry

    spend_ref[...] = jnp.zeros(spend_ref.shape, f32)
    weigh(0, weights0)
    lax.fori_loop(0, NZ // 2, both, 0)


def far_kernel(even_ref, odd_ref, hot_ref, parts_ref, far_ref, lse_ref, weights0, weights1):
    lse_ref[...] = merged([parts_ref[k] for k in range(NZ)])
    spent(NEAR, even_ref, odd_ref, hot_ref, lse_ref, far_ref, weights0, weights1)


def near_kernel(*refs):
    spent(0, *refs)


def joint_kernel(even_ref, odd_ref, hot_ref, parts_ref, far_ref, near_ref, lse_ref, *weights):
    lse_ref[...] = merged([parts_ref[k] for k in range(NZ)])
    spent(NEAR, even_ref, odd_ref, hot_ref, lse_ref, far_ref, *weights)
    spent(0, even_ref, odd_ref, hot_ref, lse_ref, near_ref, *weights)


WEIGHTS = [((NEAR, HALF), bf16)] * 2


def far_spend(even, odd, hot, parts):
    return in_vmem(
        far_kernel, [((NEAR, LANES), f32), ((ROWS, LANES), f32)], WEIGHTS, even, odd, hot, parts
    )


def joint_spend(even, odd, hot, parts):
    return in_vmem(
        joint_kernel,
        [((NEAR, LANES), f32)] * 2 + [((ROWS, LANES), f32)],
        WEIGHTS,
        even, odd, hot, parts,
    )


def near_spend(even, odd, hot, lse):
    return in_vmem(near_kernel, [((NEAR, LANES), f32)], WEIGHTS, even, odd, hot, lse)[0]


def lanes_of(rows):
    return lax.broadcasted_iota(jnp.int32, (rows, LANES), 1)


def thinned(wide, thin_ref, at, col):
    spare = lanes_of(REST) >= SLOTS
    rest = wide[THIN:OWNED]
    for j in range(3):
        moved = jnp.where(spare, pltpu.roll(rest, SLOTS - 32 * j, 1), 0.0)
        thin_ref[at + j * REST : at + (j + 1) * REST, col] = wide[j * REST : (j + 1) * REST] + moved
    thin_ref[at + 3 * REST : at + THIN, col] = wide[3 * REST : THIN]


def thin_kernel(first, second, thin_ref):
    for k in range(first.shape[0] // OWNED):
        rows = slice(k * OWNED, (k + 1) * OWNED)
        thinned(first[rows] + second[rows], thin_ref, k * THIN, slice(0, LANES))


def wide_kernel(thin_ref, wide_ref):
    lanes = lanes_of(REST)
    for k in range(thin_ref.shape[0] // THIN):
        thin = thin_ref[k * THIN : (k + 1) * THIN]
        wide_ref[k * OWNED : k * OWNED + THIN] = jnp.where(lanes_of(THIN) < SLOTS, thin, 0.0)
        rest = jnp.zeros((REST, LANES), f32)
        for j in range(3):
            moved = pltpu.roll(thin[j * REST : (j + 1) * REST], 32 + 32 * j, 1)
            rest = jnp.where((lanes >= 32 * j) & (lanes < 32 * j + 32), moved, rest)
        wide_ref[k * OWNED + THIN : (k + 1) * OWNED] = rest


def as_thin(first, second):
    rows = first.shape[0] // OWNED * THIN
    return in_vmem(thin_kernel, [((rows, LANES), f32)], [], first, second)[0]


def as_wide(thin):
    rows = thin.shape[0] // THIN * OWNED
    return in_vmem(wide_kernel, [((rows, LANES), f32)], [], thin)[0]


def landed(sources, targets, sems):
    copies = [
        pltpu.make_async_copy(source, target, sems.at[k])
        for k, (source, target) in enumerate(zip(sources, targets))
    ]
    for copy in copies:
        copy.start()
    for copy in copies:
        copy.wait()


def pack_kernel(users_hbm, slots_hbm, packs_ref, token_ref, users_ref, slots_ref, sems):
    landed((users_hbm, slots_hbm), (users_ref, slots_ref), sems)
    near = lax.axis_index("core") == 0
    users = jnp.where(near, users_ref[:, :HALF].astype(f32), users_ref[:, HALF:].astype(f32))
    half = HALF // LANES
    slots = jnp.where(near, slots_ref[:half], slots_ref[half:]).astype(f32)
    slots = jnp.concatenate([slots[r : r + 1] for r in range(half)], axis=1)
    tail = jnp.broadcast_to(slots, (PACK_ROWS - 64, HALF)).astype(bf16)
    for k in range(NZ):
        packs_ref[k, 0:64, :] = users.astype(bf16)
        packs_ref[k, 64:80, :] = tail
    token_ref[...] = slots_ref[...].astype(f32)


def state_kernel(duals_hbm, targets_hbm, after, state_ref, duals_ref, targets_ref, square, sems):
    landed((duals_hbm, targets_hbm), (duals_ref, targets_ref), sems)
    square[...] = jnp.zeros(square.shape, f32)
    square[0:SLOTS, 0:OWNED] = duals_ref[...]
    thinned(square[...].T[:OWNED], state_ref, 0, slice(0, LANES))
    square[0:SLOTS, 0:OWNED] = 0.5 / targets_ref[...]
    thinned(square[...].T[:OWNED], state_ref, 0, slice(LANES, 2 * LANES))


def from_hbm(kernel, outs, scratch, operands, *after):
    operands = [pltpu.with_memory_space_constraint(a, pltpu.HBM) for a in operands]
    hbm, vmem = pl.BlockSpec(memory_space=pltpu.HBM), pl.BlockSpec(memory_space=VMEM)
    return pl.pallas_call(
        kernel,
        in_specs=[hbm] * len(operands) + [vmem] * len(after),
        out_specs=[vmem] * len(outs),
        out_shape=[VMEM(*out) for out in outs],
        scratch_shapes=[VMEM(a.shape, a.dtype) for a in operands]
        + scratch
        + [pltpu.SemaphoreType.DMA((len(operands),))],
        compiler_params=pltpu.CompilerParams(vmem_limit_bytes=VMEM_LIMIT),
    )(*operands, *after)


def near_rows(array, x, z):
    starts = [((x + NX - s) % NX) * (NZ * OWNED) + z * OWNED for s in range(NX)]
    return jnp.concatenate([lax.dynamic_slice_in_dim(array, at, OWNED, 0) for at in starts])


def both_cores(near):
    return jnp.concatenate([near, shifted(near, "core", NC, 1)])


def over_x(owned):
    return jnp.concatenate([owned] + [shifted(owned, "x", NX, s) for s in range(1, NX)])


def shards(user_vectors, campaigns, campaign_bids, spend_targets, dual_prices, slot_index, reserve):
    x, z, y, core = (lax.axis_index(a) for a in ("x", "z", "y", "core"))
    pack, token = from_hbm(
        pack_kernel,
        [((NZ, PACK_ROWS, HALF), bf16), ((8, LANES), f32)],
        [],
        (user_vectors.T, slot_index.reshape(-1, LANES)),
    )
    pack = lax.all_to_all(pack, "z", 0, 0, tiled=True)
    token = shifted(token, "core", NC, 1)
    (state,) = from_hbm(
        state_kernel,
        [((THIN, 2 * LANES), f32)],
        [VMEM((LANES, 2 * LANES), f32)],
        (dual_prices.T, spend_targets.T),
        token,
    )
    z_late, core_late, state = lax.optimization_barrier((z, core, state))
    state = over_x(state)
    camps = both_cores(near_rows(campaigns, x, z_late))
    blank = jnp.zeros((CAMPS, SLOTS), bf16)
    camps = jnp.concatenate([blank, camps[:, :32], blank, camps[:, 32:]], axis=1)
    bids = jnp.broadcast_to(near_rows(campaign_bids, x, z_late)[:, None], (NEAR, LANES))
    bids = jnp.where(lax.broadcasted_iota(jnp.int32, (NEAR, LANES), 1) < SLOTS, bids, 0.0)
    bids = as_thin(bids, jnp.zeros((NEAR, LANES), f32))
    priced, rates = state[:, :LANES] * (bids * (-1.0 / SCALE)), state[:, LANES:] * bids

    own_reserve = (
        lax.dynamic_slice_in_dim(reserve, core_late * HALF, HALF, 0) * LOG2E
    ).reshape(1, HALF // LANES, LANES)
    at_home = (lax.broadcasted_iota(jnp.int32, (NZ, 1, 1), 0) == z) & (y == 0)
    wide_reserve = jnp.where(at_home, own_reserve, -1e30).reshape(ROWS, LANES)

    gain = 1.0
    for step in range(ITERS):
        even, odd, lse, hot = local_stats(pack, as_wide(both_cores(priced)), camps, wide_reserve)
        lse = merged([lse] + [shifted(lse, "y", NY, s) for s in range(1, NY)])
        parts = lax.all_to_all(
            jnp.broadcast_to(lse[None], (NZ, ROWS, LANES)), "z", 0, 0, tiled=True
        )
        if step + 1 < ITERS:
            far, lse = far_spend(even, odd, hot, parts)
            far = shifted(far, "core", NC, 1)
            near = near_spend(even, odd, hot, lse)
        else:
            far, near, lse = joint_spend(even, odd, hot, parts)
            far = shifted(far, "core", NC, 1)
        spend = as_thin(near, far)
        sent = (spend * SENT).astype(jnp.float16)
        if step + 1 < ITERS:
            for s in range(1, NX):
                spend = spend + jnp.roll(shifted(sent, "x", NX, s), s * THIN, 0).astype(f32) * (1.0 / SENT)
            factor = jnp.sqrt(0.5 + spend * rates)
            priced = priced * factor
            gain = factor[:THIN]
        else:
            own = spend[:THIN]
            for s in range(1, NX):
                block = shifted(sent[s * THIN : (s + 1) * THIN], "x", NX, -s)
                own = own + block.astype(f32) * (1.0 / SENT)
            gain = gain * jnp.sqrt(0.5 + own * rates[:THIN])

    home = lax.dynamic_slice_in_dim(lse.reshape(NZ, HALF), z, 1, 0).reshape(HALF)
    far = shifted(home, "core", NC, 1)
    row_lse = jnp.where(core == 0, jnp.concatenate([home, far]), jnp.concatenate([far, home]))
    fill_rate = 1.0 - jnp.exp2(reserve * LOG2E - row_lse)
    return dual_prices * as_wide(gain)[:, :SLOTS], fill_rate


def solution(mesh):
    split = Mesh(mesh.devices.reshape(NX, NZ, NY, NC), ("x", "z", "y", "core"))
    wide, narrow = ("x", "z"), ("y", "core")
    placed = (
        P(wide, None),
        P(narrow, None),
        P(narrow),
        P(narrow + wide, None),
        P(narrow + wide, None),
        P(wide),
        P(wide),
    )
    return jax.shard_map(
        shards,
        mesh=split,
        in_specs=placed,
        out_specs=(P(narrow + wide, None), P(wide)),
        check_vma=False,
    )
```
